32 devices in a mesh: ctx: 2 (over y), exp: 4 (over z), tp: 4 (over x, core).
Axes of the slice: x: 2, y: 2, z: 4, core: 2. Of those that a mesh axis runs over, the one named last changes fastest.
Arguments:
- queries: bfloat16 [256, 2048], P('ctx', ('exp', 'tp')), may hold values from -30 to 30
- rotated_key_rows: bfloat16 [256, 512], P('ctx', 'exp'), may hold values from -9 to 9
- value_vector_rows: bfloat16 [256, 512], P('ctx', 'exp'), may hold values from -6 to 6
- residual: bfloat16 [256, 4096], P(('ctx', 'exp', 'tp')), may hold values from -6 to 6
- norm_gain: float32 [4096], replicated, may hold values from 0.25 to 1.75
- out_proj: bfloat16 [2048, 4096], P(('exp', 'tp')), may hold values from -0.125 to 0.125
- expert_ids: int32 [256, 2], P('ctx'), may hold values from 0 to 3, all different within a row; in each aligned block of 128 rows (0 to 127, 128 to 255, ...) at most 128 rows name the same one
- gate_weights: float32 [256, 2], P('ctx'), may hold values from 0.2 to 1
- w_gate: bfloat16 [4, 4096, 14336], P('exp', None, ('ctx', 'tp')), may hold values from -0.09375 to 0.09375
- w_up: bfloat16 [4, 4096, 14336], P('exp', None, ('ctx', 'tp')), may hold values from -0.09375 to 0.09375
- w_down: bfloat16 [4, 14336, 4096], P('exp', ('ctx', 'tp')), may hold values from -0.046875 to 0.046875
Outputs:
- mixed: bfloat16 [256, 4096], P(('ctx', 'exp', 'tp'))
The draws below stay inside these ranges and needn't reach their ends.
Inputs may be any that keep to these rules, and one draw needn't show every extreme that they name: `expert_ids`: each row names 2 different experts. In each aligned block of 128 rows no expert is named by more than 128 rows, and in some block one expert is named by exactly 128 rows.
All inputs are finite; a program needn't handle non-finite values.
Results may differ from the reference program's by a relative error of at most 0.019.
Values may be sent and summed in bfloat16 or wider, within the bound.
A program may use at most 128 MiB of HBM per device.

```python
import math
import jax
import jax.numpy as jnp
import numpy as np
from jax import lax

D = 4096
HEAD_WIDTH = 128
QUERIES_PER_KEY = 4
HID = 14336
TOP = 2
KEY_VALUE_HEADS = 4
QUERY_HEADS = 16
EXPERTS = 4
BLK = 128
EVENT_COUNT = 256
CAPB = 128
N_CTX = 2
N_TP = 4


def shared_layout(key):
    unrotated_keys = jnp.clip(1.5 * jax.random.normal(jax.random.fold_in(key, 101), (EVENT_COUNT, KEY_VALUE_HEADS * HEAD_WIDTH), jnp.float32), -9.0, 9.0)
    return unrotated_keys


def draw_rotated_key_rows(key, part):
    unrotated_keys = shared_layout(key)
    return unrotated_keys.astype(jnp.bfloat16)


def draw_queries(key, part):
    fresh_rows = jnp.clip(1.5 * jax.random.normal(jax.random.fold_in(key, 104), (EVENT_COUNT, QUERY_HEADS * HEAD_WIDTH), jnp.float32), -9.0, 9.0)
    return fresh_rows.astype(jnp.bfloat16)


def shard_levels(rng, dims, split, smallest, top_value):
    def one(position, parts):
        steps = jax.random.uniform(jax.random.fold_in(jax.random.fold_in(rng, 6), position), (parts,), jnp.float32, smallest / len(split), top_value / len(split))
        return jnp.repeat(jnp.exp(steps), dims[position] // parts).reshape((-1,) + (1,) * (len(dims) - position - 1))

    level = one(*split[0])
    for cut in split[1:]:
        level = level * one(*cut)
    return level


def shared_out(key, own, number, rows, amount, top, bound, skew):
    ranking = jax.random.permutation(key, amount)
    heavy_load, common = shares(amount, rows * top, bound, skew, True), shares(amount, rows * top, bound, skew, False)
    places = jnp.arange(amount)

    def named(tallies, offset_by):
        used = int((tallies > 0).sum())
        fixed = max(1, used // 4)
        shifted = fixed + (places - fixed + offset_by * (used - fixed)) % max(1, amount - fixed)
        return jnp.zeros((amount,), jnp.int32).at[ranking[jnp.where(places < fixed, places, shifted)]].set(jnp.asarray(tallies, jnp.int32))

    tallies = jnp.where(number % 4 == 0, named(heavy_load, number // 4), named(common, number - number // 4 - 1))
    mixed = jax.random.permutation(jax.random.fold_in(own, 3), amount)
    donor, receiver = mixed[0:amount // 2 * 2:2], mixed[1:amount // 2 * 2:2]
    room = jnp.minimum(tallies[donor] - 1, bound - tallies[receiver]) // 2
    room = jnp.where((donor == ranking[0]) | (receiver == ranking[0]) | (tallies[receiver] == 0), 0, jnp.maximum(room, 0))
    shifted = jax.random.randint(jax.random.fold_in(own, 4), (amount // 2,), 0, 1 << 20) % (room + 1)
    tallies = tallies.at[donor].add(-shifted).at[receiver].add(shifted)
    labels = jnp.searchsorted(jnp.cumsum(tallies), jnp.arange(rows * top), side="right").astype(jnp.int32)
    grid = labels.reshape(top, rows).T
    grid = grid[jax.random.permutation(jax.random.fold_in(own, 1), rows)]
    offset_by = jax.random.randint(jax.random.fold_in(own, 2), (rows, 1), 0, top)
    return jnp.take_along_axis(grid, (jnp.arange(top)[None, :] + offset_by) % top, axis=1)


def shares(number_of, total, bound, slope, full):
    loads = [(1 << 20) // math.isqrt(rank ** slope) + 1 for rank in range(1, number_of + 1)]
    largest = bound if full else min(bound, max(-(-total // number_of), total * loads[0] // sum(loads)))
    least = 1 if total - largest >= number_of - 1 else 0
    given, spare = [largest] + [least] * (number_of - 1), total - largest - least * (number_of - 1)
    while spare > 0:
        candidates = [i for i in range(1, number_of) if given[i] < largest] or [i for i in range(1, number_of) if given[i] < bound]
        pool, remaining = sum([loads[i] for i in candidates]), spare
        for i in candidates:
            extra = min(bound - given[i], max(1, remaining * loads[i] // pool), spare)
            given[i] = given[i] + extra
            spare = spare - extra
    return np.array(given)


def gaussian(own_key, shape, width, most, pieces=(), kind=jnp.bfloat16):
    values = jax.random.normal(own_key, shape, jnp.float32) * width
    if len(pieces) > 0:
        values = shard_levels(own_key, shape, pieces, -0.22, 0.18) * values
    return jnp.clip(values, min=-most, max=most).astype(kind)


def setup_inputs(seed: int = 0) -> dict:
    keys = jax.random.split(jax.random.key(seed), 12)
    queries = draw_queries(jax.random.fold_in(keys[11], 71), 0)
    rotated_key_rows = draw_rotated_key_rows(jax.random.fold_in(keys[11], 71), 0)
    value_vector_rows = gaussian(keys[2], (EVENT_COUNT, KEY_VALUE_HEADS * HEAD_WIDTH), 1.0, 6.0, ((0, 2), (1, 4)))
    residual = gaussian(keys[3], (EVENT_COUNT, D), 1.0, 6.0, ((0, 32),))
    norm_gain = jnp.clip(1.0 + 0.15 * jax.random.normal(keys[4], (D,), jnp.float32), 0.25, 1.75)
    out_proj = gaussian(keys[5], (QUERY_HEADS * HEAD_WIDTH, D), (QUERY_HEADS * HEAD_WIDTH) ** -0.5, 0.125, ((0, 16),))
    expert_ids_keys = jax.random.split(jax.random.fold_in(keys[6], 1), EVENT_COUNT // BLK)
    expert_ids_turns = jax.random.permutation(jax.random.fold_in(keys[6], 3), EVENT_COUNT // BLK)
    expert_ids = jax.vmap(lambda own, number: shared_out(jax.random.fold_in(keys[6], 2), own, number, BLK, EXPERTS, TOP, CAPB, 2))(expert_ids_keys, expert_ids_turns).reshape((EVENT_COUNT, TOP))
    gate_weights = jnp.clip(0.2 + 0.8 * jax.random.uniform(keys[7], (EVENT_COUNT, TOP), jnp.float32) ** shard_levels(keys[7], (EVENT_COUNT, TOP), ((0, 2),), -0.2, 0.2), 0.2, 1.0)
    w_gate = gaussian(keys[8], (EXPERTS, D, HID), D ** -0.5, 0.09375, ((0, 4), (2, 8)))
    w_up = gaussian(keys[9], (EXPERTS, D, HID), D ** -0.5, 0.09375, ((0, 4), (2, 8)))
    w_down = gaussian(keys[10], (EXPERTS, HID, D), HID ** -0.5, 0.046875, ((0, 4), (1, 8)))
    return {"queries": queries, "rotated_key_rows": rotated_key_rows, "value_vector_rows": value_vector_rows, "residual": residual, "norm_gain": norm_gain, "out_proj": out_proj, "expert_ids": expert_ids, "gate_weights": gate_weights, "w_gate": w_gate, "w_up": w_up, "w_down": w_down}


def normalize(hidden_sum, norm_gain):
    mean_square = lax.optimization_barrier(jnp.mean(hidden_sum * hidden_sum, axis=-1, keepdims=True))
    return (hidden_sum * lax.rsqrt(mean_square + 1e-05) * norm_gain).astype(jnp.bfloat16)

def attend_group(head_parts):
    query_group, key_head, value_head = head_parts
    positions = jnp.arange(EVENT_COUNT, dtype=jnp.int32)
    visible = positions[None, :] <= positions[:, None]
    outputs = []
    for head_index in range(QUERIES_PER_KEY):
        scores = jnp.dot(query_group[head_index], key_head.T, preferred_element_type=jnp.float32) * HEAD_WIDTH ** (-0.5)
        scores = jnp.where(visible, scores, -1e+30)
        row_top = lax.optimization_barrier(jnp.max(scores, axis=1, keepdims=True))
        weights = jnp.where(visible, jnp.exp(scores - row_top), 0.0)
        row_sum = lax.optimization_barrier(jnp.sum(weights, axis=1, keepdims=True))
        mixed_rows = jnp.dot(weights.astype(jnp.bfloat16), value_head, preferred_element_type=jnp.float32)
        outputs.append((mixed_rows / row_sum).astype(jnp.bfloat16))
    return jnp.stack(outputs)

def reference(queries, rotated_key_rows, value_vector_rows, residual, norm_gain, out_proj, expert_ids, gate_weights, w_gate, w_up, w_down):
    grouped_query_rows = queries.reshape(EVENT_COUNT, KEY_VALUE_HEADS, QUERIES_PER_KEY, HEAD_WIDTH).transpose(1, 2, 0, 3)
    key_head_split = rotated_key_rows.reshape(EVENT_COUNT, KEY_VALUE_HEADS, HEAD_WIDTH).transpose(1, 0, 2)
    value_head_split = value_vector_rows.reshape(EVENT_COUNT, KEY_VALUE_HEADS, HEAD_WIDTH).transpose(1, 0, 2)
    attended = lax.map(attend_group, (grouped_query_rows, key_head_split, value_head_split))
    attended = attended.transpose(2, 0, 1, 3).reshape(EVENT_COUNT, QUERY_HEADS * HEAD_WIDTH)
    hidden_sum = residual.astype(jnp.float32) + jnp.dot(attended, out_proj, preferred_element_type=jnp.float32)
    normed = normalize(hidden_sum, norm_gain)
    slice_count = N_CTX * N_TP
    slice_width = HID // slice_count
    most_rows = N_CTX * CAPB

    def one_expert(expert_index):
        matches = expert_ids == expert_index
        chosen = jnp.any(matches, axis=1)
        gate_share = lax.optimization_barrier(jnp.sum(jnp.where(matches, gate_weights, 0.0), axis=1))
        picked = jnp.nonzero(chosen, size=most_rows, fill_value=0)[0].astype(jnp.int32)
        occupied = (jnp.arange(most_rows, dtype=jnp.int32) < jnp.sum(chosen.astype(jnp.int32))).astype(jnp.float32)
        picked_rows = normed[picked]
        gate_all = w_gate[expert_index]
        up_all = w_up[expert_index]
        down_all = w_down[expert_index]

        def add_slice(running, slice_index):
            first = slice_index * slice_width
            gate_part = lax.dynamic_slice_in_dim(gate_all, first, slice_width, 1)
            up_part = lax.dynamic_slice_in_dim(up_all, first, slice_width, 1)
            down_part = lax.dynamic_slice_in_dim(down_all, first, slice_width, 0)
            gate_out = jnp.dot(picked_rows, gate_part, preferred_element_type=jnp.float32)
            up_out = jnp.dot(picked_rows, up_part, preferred_element_type=jnp.float32)
            hidden = (jax.nn.silu(gate_out) * up_out).astype(jnp.bfloat16)
            slice_out = jnp.dot(hidden, down_part, preferred_element_type=jnp.float32)
            rounded = lax.optimization_barrier(slice_out.astype(jnp.bfloat16)).astype(jnp.float32)
            return (running + rounded, None)
        running, _ = lax.scan(add_slice, jnp.zeros((most_rows, D), jnp.float32), jnp.arange(slice_count, dtype=jnp.int32))
        expert_out = lax.optimization_barrier(running.astype(jnp.bfloat16)).astype(jnp.float32)
        gated = (gate_share[picked] * occupied)[:, None] * expert_out
        gated = lax.optimization_barrier(gated.astype(jnp.bfloat16)).astype(jnp.float32)
        return (picked, gated)
    picked_all, contrib = lax.map(one_expert, jnp.arange(EXPERTS, dtype=jnp.int32))
    combined = jnp.zeros((EVENT_COUNT, D), jnp.float32).at[picked_all.reshape(-1)].add(contrib.reshape(-1, D))
    return (hidden_sum + combined).astype(jnp.bfloat16)
```

```python
import functools
import math

import jax
import jax.numpy as jnp
from jax import lax
from jax.experimental import pallas as pl
from jax.experimental.pallas import tpu as pltpu
from jax.sharding import PartitionSpec as P

HEAD_WIDTH = 128


def normalize(hidden_sum, norm_gain):
    mean_square = jnp.mean(hidden_sum * hidden_sum, axis=-1, keepdims=True)
    return (hidden_sum * lax.rsqrt(mean_square + 1e-05) * norm_gain).astype(jnp.bfloat16)


def local_collectives(
    queries,
    rotated_key_rows,
    value_vector_rows,
    residual,
    norm_gain,
    out_proj,
    expert_ids,
    gate_weights,
    w_gate,
    w_up,
    w_down,
):
    block_rows = queries.shape[0]
    query_heads = queries.shape[1] // HEAD_WIDTH
    own_rows = residual.shape[0]
    query_first = lax.axis_index("ctx") * block_rows
    query_pos = query_first + jnp.arange(block_rows, dtype=jnp.int32)
    query_view = queries.reshape(block_rows, query_heads, HEAD_WIDTH)
    score_scale = HEAD_WIDTH ** (-0.5)
    row_top = jnp.full((query_heads, block_rows), -1e30, jnp.float32)
    key_piece = lax.all_gather(rotated_key_rows, "ctx", axis=0, tiled=True)
    value_piece = lax.all_gather(value_vector_rows, "ctx", axis=0, tiled=True)
    scores = (
        jnp.einsum("qhd,kd->hqk", query_view, key_piece, preferred_element_type=jnp.float32)
        * score_scale
    )
    key_pos = jnp.arange(key_piece.shape[0], dtype=jnp.int32)
    visible = (key_pos[None, :] <= query_pos[:, None])[None]
    scores = jnp.where(visible, scores, -1e30)
    new_top = jnp.maximum(row_top, jnp.max(scores, axis=2))
    weights = jnp.where(visible, jnp.exp(scores - new_top[..., None]), 0.0)
    row_sum = jnp.sum(weights, axis=2)
    weighted = jnp.einsum(
        "hqk,kd->hqd", weights.astype(jnp.bfloat16), value_piece, preferred_element_type=jnp.float32
    )
    row_top, row_sum, weighted = (new_top, row_sum, weighted)
    attended = (weighted / row_sum[..., None]).astype(jnp.bfloat16)
    attended = jnp.transpose(attended, (1, 0, 2)).reshape(block_rows, query_heads * HEAD_WIDTH)
    share_index = lax.axis_index("exp") * lax.axis_size("tp") + lax.axis_index("tp")
    row_first = share_index * own_rows
    partial_value = jnp.dot(attended, out_proj, preferred_element_type=jnp.float32)
    own_part = lax.dynamic_slice_in_dim(partial_value, row_first, own_rows, 0) + residual.astype(
        jnp.float32
    )
    placed = lax.dynamic_update_slice_in_dim(partial_value, own_part, row_first, 0)
    summed = lax.psum(placed.astype(jnp.bfloat16), ("exp", "tp")).astype(jnp.float32)
    normed_block = normalize(summed, norm_gain)
    own_sum = lax.dynamic_slice_in_dim(summed, row_first, own_rows, 0)
    my_expert = lax.axis_index("exp")
    matches = expert_ids == my_expert
    chosen = jnp.any(matches, axis=1)
    order = jnp.arange(block_rows, dtype=jnp.int32)
    before = (order[None, :] <= order[:, None]) & chosen[None, :]
    slot_rank = jnp.sum(before.astype(jnp.int32), axis=1) - 1
    gate_share = jnp.sum(jnp.where(matches, gate_weights, 0.0), axis=1)
    capacity = 2 * expert_ids.shape[1] * block_rows // lax.axis_size("exp")
    slot_ids = jnp.arange(capacity, dtype=jnp.int32)
    selector = ((slot_rank[None, :] == slot_ids[:, None]) & chosen[None, :]).astype(jnp.bfloat16)
    picked = jnp.dot(selector, normed_block, preferred_element_type=jnp.float32).astype(
        jnp.bfloat16
    )
    expert_input = lax.all_gather(picked, "ctx", axis=0, tiled=True)
    gate_matrix = w_gate[0]
    up_matrix = w_up[0]
    down_matrix = w_down[0]
    share_rows = capacity // lax.axis_size("tp")
    gate_out = jnp.dot(expert_input, gate_matrix, preferred_element_type=jnp.float32)
    up_out = jnp.dot(expert_input, up_matrix, preferred_element_type=jnp.float32)
    hidden = (jax.nn.silu(gate_out) * up_out).astype(jnp.bfloat16)
    expert_out = lax.psum_scatter(
        jnp.dot(hidden, down_matrix, preferred_element_type=jnp.float32).astype(jnp.bfloat16),
        ("ctx", "tp"),
        scatter_dimension=0,
        tiled=True,
    )
    slot_here = lax.axis_index("tp") * share_rows + jnp.arange(share_rows, dtype=jnp.int32)
    expanded_heads = jnp.where(
        (slot_rank[:, None] == slot_here[None, :]) & chosen[:, None], gate_share[:, None], 0.0
    )
    expert_wide = expert_out.astype(jnp.float32)
    combined = lax.psum_scatter(
        jnp.dot(expanded_heads, expert_wide, precision=lax.Precision.HIGHEST).astype(jnp.bfloat16),
        ("exp", "tp"),
        scatter_dimension=0,
        tiled=True,
    ).astype(jnp.float32)
    return (own_sum + combined).astype(jnp.bfloat16)


CHUNKS = 4
TILE = 256
MESH = pl.DeviceIdType.MESH
F32 = jnp.float32
BF16 = jnp.bfloat16


def pack(low, high):
    blocks = low.shape[0] // 8
    low = low.reshape(blocks, 8, low.shape[1])
    high = high.reshape(blocks, 8, high.shape[1])
    return jnp.concatenate([low, high], axis=1)


def layer_kernel(sizes, q_ref, k_ref, v_ref, res_ref, gain_ref, proj_ref, gate_ref, wg_hbm, wu_hbm, wd_hbm, out_ref,
                 wg, wu, wd, k_all, v_all, att, p1, p1_core, s1, s1_x, s2, s2_z, h, xg, xs, hid,
                 p2, p2_core, t1, t1_x, t2a, t1_y, t2b, t2a_y, t2b_x, t3, t3_z,
                 w_sem, send_sem, recv_sem):
    C, E, X, K = sizes
    rows = q_ref.shape[0]
    width = p1.shape[-1]
    half = width * CHUNKS
    ctx, exp, tp = lax.axis_index("ctx"), lax.axis_index("exp"), lax.axis_index("tp")
    x, core = lax.div(tp, K), lax.rem(tp, K)
    groups = {
        "ctx": ("ctx", ctx, 1, C, ctx),
        "exp": ("exp", exp, 1, E, exp),
        "x": ("tp", tp, K, X, x),
        "core": ("tp", tp, 1, K, core),
    }

    weights = [
        pltpu.make_async_copy(wg_hbm.at[0], wg, w_sem.at[0]),
        pltpu.make_async_copy(wu_hbm.at[0], wu, w_sem.at[1]),
        pltpu.make_async_copy(wd_hbm.at[0], wd, w_sem.at[2]),
    ]

    def partner(group, offset):
        axis, index, stride, members, digit = groups[group]
        other = lax.rem(digit + offset, members)
        return other, {axis: index + (other - digit) * stride}

    barrier = pltpu.get_barrier_semaphore()
    greeted = 0
    for group in groups:
        for offset in range(1, groups[group][3]):
            _, device = partner(group, offset)
            pl.semaphore_signal(barrier, inc=1, device_id=device, device_id_type=MESH)
            greeted += 1
    for copy in weights:
        copy.start()
    pl.semaphore_wait(barrier, greeted)

    used = [0]
    sent = []

    def exchange(group, source, target):
        copies = []
        for offset in range(1, groups[group][3]):
            other, device = partner(group, offset)
            copy = pltpu.make_async_remote_copy(
                src_ref=source(other),
                dst_ref=target(offset - 1),
                send_sem=send_sem.at[used[0]],
                recv_sem=recv_sem.at[used[0]],
                device_id=device,
                device_id_type=MESH,
            )
            used[0] += 1
            copy.start()
            copies.append(copy)
            sent.append(copy)
        return copies

    def arrived(copies):
        for copy in copies:
            copy.wait_recv()

    def total(own, slots):
        value = own[...].astype(F32)
        for i in range(slots.shape[0]):
            value = value + slots[i].astype(F32)
        return value

    chunks = range(CHUNKS)

    k_all[ctx] = k_ref[...]
    v_all[ctx] = v_ref[...]
    pending = exchange("ctx", lambda j: k_all.at[ctx], lambda i: k_all.at[ctx])
    pending += exchange("ctx", lambda j: v_all.at[ctx], lambda i: v_all.at[ctx])
    arrived(pending)

    keys = k_all[...].reshape(C * rows, HEAD_WIDTH)
    values = v_all[...].reshape(C * rows, HEAD_WIDTH)
    query_pos = ctx * rows + lax.broadcasted_iota(jnp.int32, (rows, C * rows), 0)
    visible = lax.broadcasted_iota(jnp.int32, (rows, C * rows), 1) <= query_pos
    for head in range(q_ref.shape[1] // HEAD_WIDTH):
        columns = slice(head * HEAD_WIDTH, (head + 1) * HEAD_WIDTH)
        scores = lax.dot_general(
            q_ref[:, columns], keys, (((1,), (1,)), ((), ())), preferred_element_type=F32
        ) * HEAD_WIDTH ** (-0.5)
        scores = jnp.where(visible, scores, -1e30)
        top = jnp.max(scores, axis=1, keepdims=True)
        weight = jnp.where(visible, jnp.exp(scores - top), 0.0)
        row_sum = jnp.sum(weight, axis=1, keepdims=True)
        weighted = jnp.dot(weight.astype(BF16), values, preferred_element_type=F32)
        att[:, columns] = (weighted / row_sum).astype(BF16)

    flight = []
    for ch in chunks:
        low = slice(ch * width, (ch + 1) * width)
        high = slice(half + ch * width, half + (ch + 1) * width)
        part = pack(
            jnp.dot(att[...], proj_ref[:, low], preferred_element_type=F32),
            jnp.dot(att[...], proj_ref[:, high], preferred_element_type=F32),
        )
        p1[ch] = part.astype(BF16).reshape(E, X, K, 16, width)
        flight.append(exchange("core", lambda j: p1.at[ch, :, :, j], lambda i: p1_core.at[ch, i]))
    for ch in chunks:
        arrived(flight[ch])
        s1[ch] = total(p1.at[ch, :, :, core], p1_core.at[ch]).astype(BF16)
        flight[ch] = exchange("x", lambda j: s1.at[ch, :, j], lambda i: s1_x.at[ch, i])
    for ch in chunks:
        arrived(flight[ch])
        s2[ch] = total(s1.at[ch, :, x], s1_x.at[ch]).astype(BF16)
        flight[ch] = exchange("exp", lambda j: s2.at[ch, j], lambda i: s2_z.at[ch, i])
    square = jnp.zeros((8, 1), F32)
    for ch in chunks:
        low = slice(ch * width, (ch + 1) * width)
        high = slice(half + ch * width, half + (ch + 1) * width)
        arrived(flight[ch])
        residual = jnp.concatenate([res_ref[:, low].astype(F32), res_ref[:, high].astype(F32)], axis=0)
        value = total(s2.at[ch, exp], s2_z.at[ch]) + residual
        h[ch] = value
        both = jnp.sum(value * value, axis=1, keepdims=True)
        square = square + both[:8] + both[8:]
    scale = lax.rsqrt(square / (2 * half) + 1e-05)
    scale = jnp.concatenate([scale, scale], axis=0)

    for ch in chunks:
        low = slice(ch * width, (ch + 1) * width)
        high = slice(half + ch * width, half + (ch + 1) * width)
        gain = jnp.concatenate(
            [jnp.broadcast_to(gain_ref[:, low], (8, width)), jnp.broadcast_to(gain_ref[:, high], (8, width))], axis=0
        )
        xg[ch, ctx, exp, x, core] = (h[ch] * scale * gain).astype(BF16)
        own = xg.at[ch, ctx, exp, x, core]
        flight[ch] = exchange("exp", lambda j: own, lambda i: own)
    for ch in chunks:
        arrived(flight[ch])
        own = xg.at[ch, ctx, :, x, core]
        flight[ch] = exchange("x" if ch % 2 else "ctx", lambda j: own, lambda i: own)
    for ch in chunks:
        arrived(flight[ch])
        own = xg.at[ch, ctx, :, :, core] if ch % 2 else xg.at[ch, :, :, x, core]
        flight[ch] = exchange("ctx" if ch % 2 else "x", lambda j: own, lambda i: own)
    for ch in chunks:
        arrived(flight[ch])
        own = xg.at[ch, :, :, :, core]
        flight[ch] = exchange("core", lambda j: own, lambda i: own)
    every = C * rows
    for ch in chunks:
        arrived(flight[ch])
        block = xg[ch].reshape(every // 8, 16, width).astype(F32)
        xs[:, ch * width : (ch + 1) * width] = block[:, :8].reshape(every, width).astype(BF16)
        xs[:, half + ch * width : half + (ch + 1) * width] = block[:, 8:].reshape(every, width).astype(BF16)

    weights[0].wait()
    weights[1].wait()

    @pl.loop(0, hid.shape[1] // TILE)
    def _(j):
        columns = pl.ds(pl.multiple_of(j * TILE, TILE), TILE)
        gate = jnp.dot(xs[...], wg[:, columns], preferred_element_type=F32)
        up = jnp.dot(xs[...], wu[:, columns], preferred_element_type=F32)
        hid[:, columns] = (gate / (1.0 + jnp.exp(-gate)) * up).astype(BF16)

    weights[2].wait()

    def after_core(ch):
        arrived(flight[ch])
        t1[ch] = total(p2.at[ch, :, :, :, core], p2_core.at[ch]).astype(BF16)
        if ch % 2:
            flight[ch] = exchange("ctx", lambda j: t1.at[ch, j], lambda i: t1_y.at[ch, i])
        else:
            flight[ch] = exchange("x", lambda j: t1.at[ch, :, :, j], lambda i: t1_x.at[ch, i])

    for ch in chunks:

        @pl.loop(0, width // TILE)
        def _(j):
            low = pl.ds(pl.multiple_of(ch * width + j * TILE, TILE), TILE)
            high = pl.ds(pl.multiple_of(half + ch * width + j * TILE, TILE), TILE)
            part = pack(
                jnp.dot(hid[...], wd[:, low], preferred_element_type=F32),
                jnp.dot(hid[...], wd[:, high], preferred_element_type=F32),
            )
            p2[ch, :, :, :, :, :, pl.ds(pl.multiple_of(j * TILE, TILE), TILE)] = part.astype(BF16).reshape(
                C, E, X, K, 16, TILE
            )

        flight[ch] = exchange("core", lambda j: p2.at[ch, :, :, :, j], lambda i: p2_core.at[ch, i])
        if ch:
            after_core(ch - 1)
    after_core(CHUNKS - 1)
    for ch in chunks:
        arrived(flight[ch])
        if ch % 2:
            t2b[ch] = total(t1.at[ch, ctx], t1_y.at[ch]).astype(BF16)
            flight[ch] = exchange("x", lambda j: t2b.at[ch, :, j], lambda i: t2b_x.at[ch, i])
        else:
            t2a[ch] = total(t1.at[ch, :, :, x], t1_x.at[ch]).astype(BF16)
            flight[ch] = exchange("ctx", lambda j: t2a.at[ch, j], lambda i: t2a_y.at[ch, i])
    for ch in chunks:
        arrived(flight[ch])
        if ch % 2:
            value = total(t2b.at[ch, :, x], t2b_x.at[ch])
        else:
            value = total(t2a.at[ch, ctx], t2a_y.at[ch])
        t3[ch] = (value * gate_ref[...]).astype(BF16)
        flight[ch] = exchange("exp", lambda j: t3.at[ch, j], lambda i: t3_z.at[ch, i])
    for ch in chunks:
        arrived(flight[ch])
        value = (total(t3.at[ch, exp], t3_z.at[ch]) + h[ch]).astype(BF16).astype(F32)
        out_ref[:, ch * width : (ch + 1) * width] = value[:8].astype(BF16)
        out_ref[:, half + ch * width : half + (ch + 1) * width] = value[8:].astype(BF16)
    for copy in sent:
        copy.wait_send()


def local(shape, *args):
    queries, keys, values, residual, norm_gain, out_proj, expert_ids, gate_weights, w_gate, w_up, w_down = args
    C, E, T = shape["ctx"], shape["exp"], shape["tp"]
    rows, model = queries.shape[0], residual.shape[1]
    capacity = 2 * expert_ids.shape[1] * rows // E
    if capacity < rows or T % 2 or residual.shape[0] != 8 or keys.shape[1] != HEAD_WIDTH:
        return local_collectives(*args)
    K, X = 2, T // 2
    hidden = w_gate.shape[2]
    width = model // 2 // CHUNKS

    share = jnp.sum(jnp.where(expert_ids == lax.axis_index("exp"), gate_weights, 0.0), axis=1)
    share = lax.dynamic_index_in_dim(share.reshape(E, T, 8), lax.axis_index("tp"), 1, keepdims=False)
    share = jnp.concatenate([share, share], axis=1)[:, :, None]

    vmem = pl.BlockSpec(memory_space=pltpu.VMEM)
    hbm = pl.BlockSpec(memory_space=pl.ANY)
    copies = 2 * (C - 1) + CHUNKS * (3 * (K - 1) + 3 * (X - 1) + 3 * (E - 1) + 2 * (C - 1))

    def buffer(*dims, dtype=BF16):
        return pltpu.VMEM(dims, dtype)

    tile = (16, width)
    return pl.pallas_call(
        functools.partial(layer_kernel, (C, E, X, K)),
        out_shape=jax.ShapeDtypeStruct((residual.shape[0], model), BF16),
        in_specs=[vmem] * 7 + [hbm] * 3,
        out_specs=vmem,
        scratch_shapes=[
            buffer(model, hidden),
            buffer(model, hidden),
            buffer(hidden, model),
            buffer(C, rows, HEAD_WIDTH),
            buffer(C, rows, HEAD_WIDTH),
            buffer(*queries.shape),
            buffer(CHUNKS, E, X, K, *tile),
            buffer(CHUNKS, K - 1, E, X, *tile),
            buffer(CHUNKS, E, X, *tile),
            buffer(CHUNKS, X - 1, E, *tile),
            buffer(CHUNKS, E, *tile),
            buffer(CHUNKS, E - 1, *tile),
            buffer(CHUNKS, *tile, dtype=F32),
            buffer(CHUNKS, C, E, X, K, *tile),
            buffer(C * rows, model),
            buffer(C * rows, hidden),
            buffer(CHUNKS, C, E, X, K, *tile),
            buffer(CHUNKS, K - 1, C, E, X, *tile),
            buffer(CHUNKS, C, E, X, *tile),
            buffer(CHUNKS, X - 1, C, E, *tile),
            buffer(CHUNKS, C, E, *tile),
            buffer(CHUNKS, C - 1, E, X, *tile),
            buffer(CHUNKS, E, X, *tile),
            buffer(CHUNKS, C - 1, E, *tile),
            buffer(CHUNKS, X - 1, E, *tile),
            buffer(CHUNKS, E, *tile),
            buffer(CHUNKS, E - 1, *tile),
            pltpu.SemaphoreType.DMA((3,)),
            pltpu.SemaphoreType.DMA((copies,)),
            pltpu.SemaphoreType.DMA((copies,)),
        ],
        compiler_params=pltpu.CompilerParams(
            collective_id=0, has_side_effects=True, vmem_limit_bytes=62 * 1024 * 1024
        ),
        cost_estimate=pl.CostEstimate(
            flops=6 * C * rows * model * hidden, bytes_accessed=6 * model * hidden, transcendentals=C * rows * hidden
        ),
    )(queries, keys, values, residual, norm_gain.reshape(1, model), out_proj, share, w_gate, w_up, w_down)


def solution(mesh):
    return jax.shard_map(
        functools.partial(local, dict(mesh.shape)),
        mesh=mesh,
        in_specs=(
            P("ctx", ("exp", "tp")),
            P("ctx", "exp"),
            P("ctx", "exp"),
            P(("ctx", "exp", "tp"), None),
            P(),
            P(("exp", "tp"), None),
            P("ctx", None),
            P("ctx", None),
            P("exp", None, ("ctx", "tp")),
            P("exp", None, ("ctx", "tp")),
            P("exp", ("ctx", "tp"), None),
        ),
        out_specs=P(("ctx", "exp", "tp"), None),
        check_vma=False,
    )
```

```python
import functools
import math

import jax
import jax.numpy as jnp
from jax import lax
from jax.experimental import pallas as pl
from jax.experimental.pallas import tpu as pltpu
from jax.sharding import PartitionSpec as P

HEAD_WIDTH = 128


def normalize(hidden_sum, norm_gain):
    mean_square = jnp.mean(hidden_sum * hidden_sum, axis=-1, keepdims=True)
    return (hidden_sum * lax.rsqrt(mean_square + 1e-05) * norm_gain).astype(jnp.bfloat16)


def local_collectives(
    queries,
    rotated_key_rows,
    value_vector_rows,
    residual,
    norm_gain,
    out_proj,
    expert_ids,
    gate_weights,
    w_gate,
    w_up,
    w_down,
):
    block_rows = queries.shape[0]
    query_heads = queries.shape[1] // HEAD_WIDTH
    own_rows = residual.shape[0]
    query_first = lax.axis_index("ctx") * block_rows
    query_pos = query_first + jnp.arange(block_rows, dtype=jnp.int32)
    query_view = queries.reshape(block_rows, query_heads, HEAD_WIDTH)
    score_scale = HEAD_WIDTH ** (-0.5)
    row_top = jnp.full((query_heads, block_rows), -1e30, jnp.float32)
    key_piece = lax.all_gather(rotated_key_rows, "ctx", axis=0, tiled=True)
    value_piece = lax.all_gather(value_vector_rows, "ctx", axis=0, tiled=True)
    scores = (
        jnp.einsum("qhd,kd->hqk", query_view, key_piece, preferred_element_type=jnp.float32)
        * score_scale
    )
    key_pos = jnp.arange(key_piece.shape[0], dtype=jnp.int32)
    visible = (key_pos[None, :] <= query_pos[:, None])[None]
    scores = jnp.where(visible, scores, -1e30)
    new_top = jnp.maximum(row_top, jnp.max(scores, axis=2))
    weights = jnp.where(visible, jnp.exp(scores - new_top[..., None]), 0.0)
    row_sum = jnp.sum(weights, axis=2)
    weighted = jnp.einsum(
        "hqk,kd->hqd", weights.astype(jnp.bfloat16), value_piece, preferred_element_type=jnp.float32
    )
    row_top, row_sum, weighted = (new_top, row_sum, weighted)
    attended = (weighted / row_sum[..., None]).astype(jnp.bfloat16)
    attended = jnp.transpose(attended, (1, 0, 2)).reshape(block_rows, query_heads * HEAD_WIDTH)
    share_index = lax.axis_index("exp") * lax.axis_size("tp") + lax.axis_index("tp")
    row_first = share_index * own_rows
    partial_value = jnp.dot(attended, out_proj, preferred_element_type=jnp.float32)
    own_part = lax.dynamic_slice_in_dim(partial_value, row_first, own_rows, 0) + residual.astype(
        jnp.float32
    )
    placed = lax.dynamic_update_slice_in_dim(partial_value, own_part, row_first, 0)
    summed = lax.psum(placed.astype(jnp.bfloat16), ("exp", "tp")).astype(jnp.float32)
    normed_block = normalize(summed, norm_gain)
    own_sum = lax.dynamic_slice_in_dim(summed, row_first, own_rows, 0)
    my_expert = lax.axis_index("exp")
    matches = expert_ids == my_expert
    chosen = jnp.any(matches, axis=1)
    order = jnp.arange(block_rows, dtype=jnp.int32)
    before = (order[None, :] <= order[:, None]) & chosen[None, :]
    slot_rank = jnp.sum(before.astype(jnp.int32), axis=1) - 1
    gate_share = jnp.sum(jnp.where(matches, gate_weights, 0.0), axis=1)
    capacity = 2 * expert_ids.shape[1] * block_rows // lax.axis_size("exp")
    slot_ids = jnp.arange(capacity, dtype=jnp.int32)
    selector = ((slot_rank[None, :] == slot_ids[:, None]) & chosen[None, :]).astype(jnp.bfloat16)
    picked = jnp.dot(selector, normed_block, preferred_element_type=jnp.float32).astype(
        jnp.bfloat16
    )
    expert_input = lax.all_gather(picked, "ctx", axis=0, tiled=True)
    gate_matrix = w_gate[0]
    up_matrix = w_up[0]
    down_matrix = w_down[0]
    share_rows = capacity // lax.axis_size("tp")
    gate_out = jnp.dot(expert_input, gate_matrix, preferred_element_type=jnp.float32)
    up_out = jnp.dot(expert_input, up_matrix, preferred_element_type=jnp.float32)
    hidden = (jax.nn.silu(gate_out) * up_out).astype(jnp.bfloat16)
    expert_out = lax.psum_scatter(
        jnp.dot(hidden, down_matrix, preferred_element_type=jnp.float32).astype(jnp.bfloat16),
        ("ctx", "tp"),
        scatter_dimension=0,
        tiled=True,
    )
    slot_here = lax.axis_index("tp") * share_rows + jnp.arange(share_rows, dtype=jnp.int32)
    expanded_heads = jnp.where(
        (slot_rank[:, None] == slot_here[None, :]) & chosen[:, None], gate_share[:, None], 0.0
    )
    expert_wide = expert_out.astype(jnp.float32)
    combined = lax.psum_scatter(
        jnp.dot(expanded_heads, expert_wide, precision=lax.Precision.HIGHEST).astype(jnp.bfloat16),
        ("exp", "tp"),
        scatter_dimension=0,
        tiled=True,
    ).astype(jnp.float32)
    return (own_sum + combined).astype(jnp.bfloat16)


CHUNKS = 8
TILE = 256
MESH = pl.DeviceIdType.MESH
F32 = jnp.float32
BF16 = jnp.bfloat16


def pack(low, high):
    blocks = low.shape[0] // 8
    low = low.reshape(blocks, 8, low.shape[1])
    high = high.reshape(blocks, 8, high.shape[1])
    return jnp.concatenate([low, high], axis=1)


def layer_kernel(sizes, q_ref, k_ref, v_ref, res_ref, gain_ref, proj_ref, gate_ref, wg_hbm, wu_hbm, wd_hbm, out_ref,
                 wg, wu, wd, k_all, v_all, att, p1, p1_core, s1, s1_x, s2, s2_z, h, xg, xs, hid,
                 p2, p2_core, t1, t1_x, t2a, t1_y, t2b, t2a_y, t2b_x, t3, t3_z,
                 w_sem, send_sem, recv_sem):
    C, E, X, K = sizes
    rows = q_ref.shape[0]
    width = p1.shape[-1]
    half = width * CHUNKS
    ctx, exp, tp = lax.axis_index("ctx"), lax.axis_index("exp"), lax.axis_index("tp")
    x, core = lax.div(tp, K), lax.rem(tp, K)
    groups = {
        "ctx": ("ctx", ctx, 1, C, ctx),
        "exp": ("exp", exp, 1, E, exp),
        "x": ("tp", tp, K, X, x),
        "core": ("tp", tp, 1, K, core),
    }

    weights = [
        pltpu.make_async_copy(wg_hbm.at[0], wg, w_sem.at[0]),
        pltpu.make_async_copy(wu_hbm.at[0], wu, w_sem.at[1]),
        pltpu.make_async_copy(wd_hbm.at[0], wd, w_sem.at[2]),
    ]

    def partner(group, offset):
        axis, index, stride, members, digit = groups[group]
        other = lax.rem(digit + offset, members)
        return other, {axis: index + (other - digit) * stride}

    barrier = pltpu.get_barrier_semaphore()
    greeted = 0
    for group in groups:
        for offset in range(1, groups[group][3]):
            _, device = partner(group, offset)
            pl.semaphore_signal(barrier, inc=1, device_id=device, device_id_type=MESH)
            greeted += 1
    for copy in weights:
        copy.start()
    pl.semaphore_wait(barrier, greeted)

    used = [0]
    sent = []

    def exchange(group, source, target):
        copies = []
        for offset in range(1, groups[group][3]):
            other, device = partner(group, offset)
            copy = pltpu.make_async_remote_copy(
                src_ref=source(other),
                dst_ref=target(offset - 1),
                send_sem=send_sem.at[used[0]],
                recv_sem=recv_sem.at[used[0]],
                device_id=device,
                device_id_type=MESH,
            )
            used[0] += 1
            copy.start()
            copies.append(copy)
            sent.append(copy)
        return copies

    def arrived(copies):
        for copy in copies:
            copy.wait_recv()

    def total(own, slots):
        value = own[...].astype(F32)
        for i in range(slots.shape[0]):
            value = value + slots[i].astype(F32)
        return value

    chunks = range(CHUNKS)

    k_all[ctx] = k_ref[...]
    v_all[ctx] = v_ref[...]
    pending = exchange("ctx", lambda j: k_all.at[ctx], lambda i: k_all.at[ctx])
    pending += exchange("ctx", lambda j: v_all.at[ctx], lambda i: v_all.at[ctx])
    arrived(pending)

    keys = k_all[...].reshape(C * rows, HEAD_WIDTH)
    values = v_all[...].reshape(C * rows, HEAD_WIDTH)
    query_pos = ctx * rows + lax.broadcasted_iota(jnp.int32, (rows, C * rows), 0)
    visible = lax.broadcasted_iota(jnp.int32, (rows, C * rows), 1) <= query_pos
    for head in range(q_ref.shape[1] // HEAD_WIDTH):
        columns = slice(head * HEAD_WIDTH, (head + 1) * HEAD_WIDTH)
        scores = lax.dot_general(
            q_ref[:, columns], keys, (((1,), (1,)), ((), ())), preferred_element_type=F32
        ) * HEAD_WIDTH ** (-0.5)
        scores = jnp.where(visible, scores, -1e30)
        top = jnp.max(scores, axis=1, keepdims=True)
        weight = jnp.where(visible, jnp.exp(scores - top), 0.0)
        row_sum = jnp.sum(weight, axis=1, keepdims=True)
        weighted = jnp.dot(weight.astype(BF16), values, preferred_element_type=F32)
        att[:, columns] = (weighted / row_sum).astype(BF16)

    flight = []
    for ch in chunks:
        low = slice(ch * width, (ch + 1) * width)
        high = slice(half + ch * width, half + (ch + 1) * width)
        part = pack(
            jnp.dot(att[...], proj_ref[:, low], preferred_element_type=F32),
            jnp.dot(att[...], proj_ref[:, high], preferred_element_type=F32),
        )
        p1[ch] = part.astype(BF16).reshape(E, X, K, 16, width)
        flight.append(exchange("core", lambda j: p1.at[ch, :, :, j], lambda i: p1_core.at[ch, i]))
    for ch in chunks:
        arrived(flight[ch])
        s1[ch] = total(p1.at[ch, :, :, core], p1_core.at[ch]).astype(BF16)
        flight[ch] = exchange("x", lambda j: s1.at[ch, :, j], lambda i: s1_x.at[ch, i])
    for ch in chunks:
        arrived(flight[ch])
        s2[ch] = total(s1.at[ch, :, x], s1_x.at[ch]).astype(BF16)
        flight[ch] = exchange("exp", lambda j: s2.at[ch, j], lambda i: s2_z.at[ch, i])
    square = jnp.zeros((8, 1), F32)
    for ch in chunks:
        low = slice(ch * width, (ch + 1) * width)
        high = slice(half + ch * width, half + (ch + 1) * width)
        arrived(flight[ch])
        residual = jnp.concatenate([res_ref[:, low].astype(F32), res_ref[:, high].astype(F32)], axis=0)
        value = total(s2.at[ch, exp], s2_z.at[ch]) + residual
        h[ch] = value
        both = jnp.sum(value * value, axis=1, keepdims=True)
        square = square + both[:8] + both[8:]
    scale = lax.rsqrt(square / (2 * half) + 1e-05)
    scale = jnp.concatenate([scale, scale], axis=0)

    for ch in chunks:
        low = slice(ch * width, (ch + 1) * width)
        high = slice(half + ch * width, half + (ch + 1) * width)
        gain = jnp.concatenate(
            [jnp.broadcast_to(gain_ref[:, low], (8, width)), jnp.broadcast_to(gain_ref[:, high], (8, width))], axis=0
        )
        xg[ch, ctx, exp, x, core] = (h[ch] * scale * gain).astype(BF16)
        own = xg.at[ch, ctx, exp, x, core]
        flight[ch] = exchange("exp", lambda j: own, lambda i: own)
    for ch in chunks:
        arrived(flight[ch])
        own = xg.at[ch, ctx, :, x, core]
        flight[ch] = exchange("x" if ch % 2 else "ctx", lambda j: own, lambda i: own)
    for ch in chunks:
        arrived(flight[ch])
        own = xg.at[ch, ctx, :, :, core] if ch % 2 else xg.at[ch, :, :, x, core]
        flight[ch] = exchange("ctx" if ch % 2 else "x", lambda j: own, lambda i: own)
    for ch in chunks:
        arrived(flight[ch])
        own = xg.at[ch, :, :, :, core]
        flight[ch] = exchange("core", lambda j: own, lambda i: own)
    every = C * rows
    for ch in chunks:
        arrived(flight[ch])
        block = xg[ch].reshape(every // 8, 16, width).astype(F32)
        xs[:, ch * width : (ch + 1) * width] = block[:, :8].reshape(every, width).astype(BF16)
        xs[:, half + ch * width : half + (ch + 1) * width] = block[:, 8:].reshape(every, width).astype(BF16)

    weights[0].wait()
    weights[1].wait()

    @pl.loop(0, hid.shape[1] // TILE)
    def _(j):
        columns = pl.ds(pl.multiple_of(j * TILE, TILE), TILE)
        gate = jnp.dot(xs[...], wg[:, columns], preferred_element_type=F32)
        up = jnp.dot(xs[...], wu[:, columns], preferred_element_type=F32)
        hid[:, columns] = (gate / (1.0 + jnp.exp(-gate)) * up).astype(BF16)

    weights[2].wait()

    def after_core(ch):
        arrived(flight[ch])
        t1[ch] = total(p2.at[ch, :, :, :, core], p2_core.at[ch]).astype(BF16)
        if ch % 2:
            flight[ch] = exchange("ctx", lambda j: t1.at[ch, j], lambda i: t1_y.at[ch, i])
        else:
            flight[ch] = exchange("x", lambda j: t1.at[ch, :, :, j], lambda i: t1_x.at[ch, i])

    for ch in chunks:

        @pl.loop(0, width // TILE)
        def _(j):
            low = pl.ds(pl.multiple_of(ch * width + j * TILE, TILE), TILE)
            high = pl.ds(pl.multiple_of(half + ch * width + j * TILE, TILE), TILE)
            part = pack(
                jnp.dot(hid[...], wd[:, low], preferred_element_type=F32),
                jnp.dot(hid[...], wd[:, high], preferred_element_type=F32),
            )
            p2[ch, :, :, :, :, :, pl.ds(pl.multiple_of(j * TILE, TILE), TILE)] = part.astype(BF16).reshape(
                C, E, X, K, 16, TILE
            )

        flight[ch] = exchange("core", lambda j: p2.at[ch, :, :, :, j], lambda i: p2_core.at[ch, i])
        if ch:
            after_core(ch - 1)
    after_core(CHUNKS - 1)
    for ch in chunks:
        arrived(flight[ch])
        if ch % 2:
            t2b[ch] = total(t1.at[ch, ctx], t1_y.at[ch]).astype(BF16)
            flight[ch] = exchange("x", lambda j: t2b.at[ch, :, j], lambda i: t2b_x.at[ch, i])
        else:
            t2a[ch] = total(t1.at[ch, :, :, x], t1_x.at[ch]).astype(BF16)
            flight[ch] = exchange("ctx", lambda j: t2a.at[ch, j], lambda i: t2a_y.at[ch, i])
    for ch in chunks:
        arrived(flight[ch])
        if ch % 2:
            value = total(t2b.at[ch, :, x], t2b_x.at[ch])
        else:
            value = total(t2a.at[ch, ctx], t2a_y.at[ch])
        t3[ch] = (value * gate_ref[...]).astype(BF16)
        flight[ch] = exchange("exp", lambda j: t3.at[ch, j], lambda i: t3_z.at[ch, i])
    for ch in chunks:
        arrived(flight[ch])
        value = (total(t3.at[ch, exp], t3_z.at[ch]) + h[ch]).astype(BF16).astype(F32)
        out_ref[:, ch * width : (ch + 1) * width] = value[:8].astype(BF16)
        out_ref[:, half + ch * width : half + (ch + 1) * width] = value[8:].astype(BF16)
    for copy in sent:
        copy.wait_send()


def local(shape, *args):
    queries, keys, values, residual, norm_gain, out_proj, expert_ids, gate_weights, w_gate, w_up, w_down = args
    C, E, T = shape["ctx"], shape["exp"], shape["tp"]
    rows, model = queries.shape[0], residual.shape[1]
    capacity = 2 * expert_ids.shape[1] * rows // E
    if capacity < rows or T % 2 or residual.shape[0] != 8 or keys.shape[1] != HEAD_WIDTH:
        return local_collectives(*args)
    K, X = 2, T // 2
    hidden = w_gate.shape[2]
    width = model // 2 // CHUNKS

    share = jnp.sum(jnp.where(expert_ids == lax.axis_index("exp"), gate_weights, 0.0), axis=1)
    share = lax.dynamic_index_in_dim(share.reshape(E, T, 8), lax.axis_index("tp"), 1, keepdims=False)
    share = jnp.concatenate([share, share], axis=1)[:, :, None]

    vmem = pl.BlockSpec(memory_space=pltpu.VMEM)
    hbm = pl.BlockSpec(memory_space=pl.ANY)
    copies = 2 * (C - 1) + CHUNKS * (3 * (K - 1) + 3 * (X - 1) + 3 * (E - 1) + 2 * (C - 1))

    def buffer(*dims, dtype=BF16):
        return pltpu.VMEM(dims, dtype)

    tile = (16, width)
    return pl.pallas_call(
        functools.partial(layer_kernel, (C, E, X, K)),
        out_shape=jax.ShapeDtypeStruct((residual.shape[0], model), BF16),
        in_specs=[vmem] * 7 + [hbm] * 3,
        out_specs=vmem,
        scratch_shapes=[
            buffer(model, hidden),
            buffer(model, hidden),
            buffer(hidden, model),
            buffer(C, rows, HEAD_WIDTH),
            buffer(C, rows, HEAD_WIDTH),
            buffer(*queries.shape),
            buffer(CHUNKS, E, X, K, *tile),
            buffer(CHUNKS, K - 1, E, X, *tile),
            buffer(CHUNKS, E, X, *tile),
            buffer(CHUNKS, X - 1, E, *tile),
            buffer(CHUNKS, E, *tile),
            buffer(CHUNKS, E - 1, *tile),
            buffer(CHUNKS, *tile, dtype=F32),
            buffer(CHUNKS, C, E, X, K, *tile),
            buffer(C * rows, model),
            buffer(C * rows, hidden),
            buffer(CHUNKS, C, E, X, K, *tile),
            buffer(CHUNKS, K - 1, C, E, X, *tile),
            buffer(CHUNKS, C, E, X, *tile),
            buffer(CHUNKS, X - 1, C, E, *tile),
            buffer(CHUNKS, C, E, *tile),
            buffer(CHUNKS, C - 1, E, X, *tile),
            buffer(CHUNKS, E, X, *tile),
            buffer(CHUNKS, C - 1, E, *tile),
            buffer(CHUNKS, X - 1, E, *tile),
            buffer(CHUNKS, E, *tile),
            buffer(CHUNKS, E - 1, *tile),
            pltpu.SemaphoreType.DMA((3,)),
            pltpu.SemaphoreType.DMA((copies,)),
            pltpu.SemaphoreType.DMA((copies,)),
        ],
        compiler_params=pltpu.CompilerParams(
            collective_id=0, has_side_effects=True, vmem_limit_bytes=62 * 1024 * 1024
        ),
        cost_estimate=pl.CostEstimate(
            flops=6 * C * rows * model * hidden, bytes_accessed=6 * model * hidden, transcendentals=C * rows * hidden
        ),
    )(queries, keys, values, residual, norm_gain.reshape(1, model), out_proj, share, w_gate, w_up, w_down)


def solution(mesh):
    return jax.shard_map(
        functools.partial(local, dict(mesh.shape)),
        mesh=mesh,
        in_specs=(
            P("ctx", ("exp", "tp")),
            P("ctx", "exp"),
            P("ctx", "exp"),
            P(("ctx", "exp", "tp"), None),
            P(),
            P(("exp", "tp"), None),
            P("ctx", None),
            P("ctx", None),
            P("exp", None, ("ctx", "tp")),
            P("exp", None, ("ctx", "tp")),
            P("exp", ("ctx", "tp"), None),
        ),
        out_specs=P(("ctx", "exp", "tp"), None),
        check_vma=False,
    )
```
